32 devices in a mesh: groups: 2 (over y), row: 4 (over x, core), col: 4 (over z).
Axes of the slice: x: 2, y: 2, z: 4, core: 2. Of those that a mesh axis runs over, the one named last changes fastest.
Arguments:
- trial_panel: bfloat16 [8, 4, 512, 256], P(('groups', 'col'), 'row'), parts along dimension 0, may hold values from -6 to 6
- tile_values: bfloat16 [8, 4, 128, 128, 128], P(('groups', 'row'), 'col'), parts along dimension 0, as said below
- tile_rows: int32 [8, 4, 128], P(('groups', 'row'), 'col'), parts along dimension 0, may hold values from 0 to 15, as said below
- tile_cols: int32 [8, 4, 128], P(('groups', 'row'), 'col'), parts along dimension 0, may hold values from 0 to 15, as said below
- tile_counts: int32 [8, 4], P(('groups', 'row'), 'col'), parts along dimension 0, may hold values from 32 to 128, as said below
Outputs:
- filtered_panel: float32 [8, 4, 512, 256], P(('groups', 'row'), 'col'), parts along dimension 0
The draws below stay inside these ranges and needn't reach their ends.
There are 2 independent parts, one for each index of `groups`. The reference program is written for one: setup_inputs(seed, part) draws one part's arguments, and reference() takes and returns one part's arrays. A program takes and returns all parts, laid end to end along the dimension named above; each array names one. Nothing has to cross between parts.
Inputs may be any that keep to these rules, and one draw needn't show every extreme that they name: `tile_rows`: cell (c, r) lists in each slot the tile of the same slot of cell (r, c) mirrored (rows and columns swapped); on a cell with r == c slot s + 64 mirrors slot s. Within a cell the slots name distinct positions (block row, block column), except that on a cell with r == c slots s and s + 64 share a position when it lies on the diagonal. `tile_cols`: mirrored as tile_rows is. `tile_counts`: the used slots are the first ones; cells (r, c) and (c, r) use equally many; cells with r == c use all 128. `tile_values`: the tile of a slot of cell (c, r) is the transpose of the tile of the same slot of cell (r, c); on a cell with r == c the tile of slot s + 64 is the transpose of that of slot s.
All inputs are finite; a program needn't handle non-finite values.
Results may differ from the reference program's by a relative error of at most 0.02.
Values may be sent and summed in bfloat16 or wider, within the bound.
A program may use at most 64 MiB of HBM per device.

```python
import jax
import jax.numpy as jnp
from jax import lax

TILE_SIZE = 128
VECTORS = 256
GROUP_BLOCKS = 16
SLOTS = 128
DEGREE = 3
GRID_SIDE = 4
PIECE_ROWS = 512


def slot_layout(key):
    first_key, third_key = jax.random.split(key, 2)
    positions = GROUP_BLOCKS * GROUP_BLOCKS
    noise = jax.random.randint(first_key, (GRID_SIDE, GRID_SIDE, positions), 0, 2 ** 18).astype(jnp.int32)
    place_iota = jnp.arange(positions).astype(jnp.int32)
    place_row = place_iota // GROUP_BLOCKS
    place_col = place_iota % GROUP_BLOCKS
    below = (place_row > place_col)[None, None, :]
    same_cell = (jnp.arange(GRID_SIDE)[:, None] == jnp.arange(GRID_SIDE)[None, :])[:, :, None]
    penalty = jnp.where(below & same_cell, 2 ** 30, 0).astype(jnp.int32)
    scores = noise * positions + place_iota[None, None, :] + penalty
    order = jnp.argsort(scores, axis=2)[:, :, :SLOTS].astype(jnp.int32)
    row_draw = (order // GROUP_BLOCKS).astype(jnp.int32)
    col_draw = (order % GROUP_BLOCKS).astype(jnp.int32)
    count_draw = jax.random.randint(third_key, (GRID_SIDE, GRID_SIDE), SLOTS // 4, SLOTS // 2 + 1).astype(jnp.int32)
    grid_rows = jnp.arange(GRID_SIDE)[:, None]
    grid_cols = jnp.arange(GRID_SIDE)[None, :]
    upper = (grid_rows < grid_cols)[:, :, None]
    lower = (grid_rows > grid_cols)[:, :, None]
    half_slots = SLOTS // 2
    row_mirror = jnp.concatenate([row_draw[:, :, :half_slots], col_draw[:, :, :half_slots]], axis=2)
    col_mirror = jnp.concatenate([col_draw[:, :, :half_slots], row_draw[:, :, :half_slots]], axis=2)
    rows_out = jnp.where(upper, row_draw, jnp.where(lower, jnp.swapaxes(col_draw, 0, 1), row_mirror))
    cols_out = jnp.where(upper, col_draw, jnp.where(lower, jnp.swapaxes(row_draw, 0, 1), col_mirror))
    counts_upper = jnp.where(grid_rows < grid_cols, count_draw, count_draw.T)
    counts_out = jnp.where(grid_rows == grid_cols, SLOTS, counts_upper).astype(jnp.int32)
    return (rows_out.astype(jnp.int32), cols_out.astype(jnp.int32), counts_out)


def draw_tile_rows(key, part):
    rows_out, cols_out, counts_out = slot_layout(key)
    return rows_out


def draw_tile_cols(key, part):
    rows_out, cols_out, counts_out = slot_layout(key)
    return cols_out


def draw_tile_counts(key, part):
    rows_out, cols_out, counts_out = slot_layout(key)
    return counts_out


def draw_tile_values(key, part):
    key = jax.random.fold_in(key, 11)
    fan_total = TILE_SIZE * (SLOTS + (GRID_SIDE - 1) * (3 * SLOTS // 8)) / GROUP_BLOCKS
    spread = 1.0 / fan_total ** 0.5
    shape_all = (GRID_SIDE, GRID_SIDE, SLOTS, TILE_SIZE, TILE_SIZE)
    base = jax.random.normal(key, shape_all, jnp.float32) * spread
    grid_rows = jnp.arange(GRID_SIDE)[:, None]
    grid_cols = jnp.arange(GRID_SIDE)[None, :]
    upper = (grid_rows < grid_cols)[:, :, None, None, None]
    lower = (grid_rows > grid_cols)[:, :, None, None, None]
    half_slots = SLOTS // 2
    mirrored = jnp.swapaxes(jnp.swapaxes(base, 0, 1), 3, 4)
    diagonal_form = jnp.concatenate([base[:, :, :half_slots], jnp.swapaxes(base[:, :, :half_slots], 3, 4)], axis=2)
    values = jnp.where(upper, base, jnp.where(lower, mirrored, diagonal_form))
    return values.astype(jnp.bfloat16)


def steps_of(stream_key, extent, pieces, least, top_value):
    gain, own = 1.0, jax.random.fold_in(stream_key, 6)
    for position, blocks in pieces:
        steps = jnp.exp(jax.random.uniform(jax.random.fold_in(own, position), (blocks,), jnp.float32, least / len(pieces), top_value / len(pieces)))
        gain = gain * jnp.repeat(steps, extent[position] // blocks).reshape([-1 if axis == position else 1 for axis in range(len(extent))])
    return gain


def scatter_about(key, extent, scale, reach, cuts=(), held_as=jnp.bfloat16):
    entries = scale * jax.random.normal(key, extent, jnp.float32)
    if cuts:
        entries = entries * steps_of(key, extent, cuts, -0.22, 0.18)
    return jnp.clip(entries, -reach, reach).astype(held_as)


def setup_inputs(seed: int = 0, part: int = 0) -> dict:
    key_list = jax.random.split(jax.random.key(seed), 6)
    part_keys = jax.random.split(jax.random.fold_in(key_list[5], part), 6)
    return {
        "trial_panel": scatter_about(part_keys[0], (GRID_SIDE, GRID_SIDE, PIECE_ROWS, VECTORS), 1.0, 6.0, ((0, 4), (1, 4))),
        "tile_values": draw_tile_values(jax.random.fold_in(jax.random.fold_in(key_list[5], part), 71), part),
        "tile_rows": draw_tile_rows(jax.random.fold_in(jax.random.fold_in(key_list[5], part), 71), part),
        "tile_cols": draw_tile_cols(jax.random.fold_in(jax.random.fold_in(key_list[5], part), 71), part),
        "tile_counts": draw_tile_counts(jax.random.fold_in(jax.random.fold_in(key_list[5], part), 71), part),
    }


filter_center = 0.5
filter_radius = 1.5


def cell_product(cell_tiles, rows_index, cols_index, used_count, source, on_diagonal):
    picked = jnp.take(source, cols_index, axis=0).astype(jnp.float32)
    products = jnp.einsum("sab,sbw->saw", cell_tiles.astype(jnp.float32), picked)
    products = lax.optimization_barrier(products.astype(jnp.bfloat16)).astype(jnp.float32)
    active = (jnp.arange(SLOTS).astype(jnp.int32) < used_count).astype(jnp.float32)
    summed = jax.ops.segment_sum(products * active[:, None, None], rows_index, num_segments=GROUP_BLOCKS)
    summed = summed - filter_center * on_diagonal * source.astype(jnp.float32)
    rounded = lax.optimization_barrier(summed.astype(jnp.bfloat16))
    return rounded.astype(jnp.float32)


def filtered_sum(panel_rounded, tile_values, tile_rows, tile_cols, tile_counts):
    def grid_line(group_index):
        def advance(running, other_index):
            on_diagonal = (group_index == other_index).astype(jnp.float32)
            part = cell_product(tile_values[group_index, other_index], tile_rows[group_index, other_index],
                                tile_cols[group_index, other_index], tile_counts[group_index, other_index],
                                panel_rounded[other_index], on_diagonal)
            return running + part, None

        start_sum = jnp.zeros((GROUP_BLOCKS, TILE_SIZE, VECTORS), jnp.float32)
        running, _ = lax.scan(advance, start_sum, jnp.arange(GRID_SIDE).astype(jnp.int32))
        return running

    return lax.map(grid_line, jnp.arange(GRID_SIDE).astype(jnp.int32))


def reference(trial_panel, tile_values, tile_rows, tile_cols, tile_counts):
    grouped = trial_panel.reshape(GRID_SIDE, GROUP_BLOCKS, TILE_SIZE, VECTORS)
    previous = grouped.astype(jnp.float32)
    current = filtered_sum(grouped, tile_values, tile_rows, tile_cols, tile_counts) / filter_radius
    for degree in range(1, DEGREE):
        rounded = current.astype(jnp.bfloat16)
        updated = (2.0 / filter_radius) * filtered_sum(rounded, tile_values, tile_rows, tile_cols, tile_counts) - previous
        previous, current = current, updated
    return current.reshape(GRID_SIDE, GRID_SIDE, PIECE_ROWS, VECTORS)
```

```python
import functools

import jax
import jax.numpy as jnp
from jax import lax
from jax.experimental import pallas as pl
from jax.experimental.pallas import tpu as pltpu
from jax.sharding import PartitionSpec as P

MESH = pl.DeviceIdType.MESH
LANES = 128
filter_center = 0.5
filter_radius = 1.5
F32 = jnp.float32
BF16 = jnp.bfloat16


class Line:
    def __init__(self, size, place, peer):
        self.size, self.place, self.peer = size, place, peer

    def copy(self, buf, side, piece, send, recv, slot=None):
        target = self.peer(1 if side == 0 else -1)
        ref = buf.at[piece] if slot is None else buf.at[side, piece]
        return pltpu.make_async_remote_copy(
            src_ref=ref, dst_ref=ref, send_sem=send.at[side, piece], recv_sem=recv.at[side, piece],
            device_id=target, device_id_type=MESH)

    def arrival(self, buf, side, piece, send, recv, slot=None):
        self.copy(buf, side, piece, send, recv, slot).wait_recv()

    def sum_moves(self, t):
        n, i = self.size, self.place
        j = n - 1 - i
        return ((0, (t >= i) & (t <= n - 2), n - 1 - t + i, i > 0),
                (1, (t >= j) & (t <= n - 2), t - j, i < n - 1))

    def sum_step(self, t, buf, part, send, recv):
        for side, active, piece, inner in self.sum_moves(t):
            @pl.when(active)
            def _():
                @pl.when(inner)
                def _():
                    self.arrival(buf, side, piece, send, recv, 1)
                    buf[side, piece] = (part[piece] + buf[side, piece].astype(F32)).astype(BF16)

                @pl.when(jnp.logical_not(inner))
                def _():
                    buf[side, piece] = part[piece].astype(BF16)

                self.copy(buf, side, piece, send, recv, 1).start()

    def sum_finish(self, buf, part, send, recv, total):
        i = self.place
        total[...] = part[i]
        for side, inner in ((0, i > 0), (1, i < self.size - 1)):
            @pl.when(inner)
            def _():
                self.arrival(buf, side, i, send, recv, 1)
                total[...] += buf[side, i].astype(F32)

    def sum_drain(self, buf, send, recv):
        for t in range(self.size - 1):
            for side, active, piece, _ in self.sum_moves(t):
                @pl.when(active)
                def _():
                    self.copy(buf, side, piece, send, recv, 1).wait_send()

    def spread_moves(self, s):
        n, i = self.size, self.place
        return ((0, i - s >= 0, i - s, i < n - 1), (1, i + s <= n - 1, i + s, i > 0))

    def spread_step(self, s, buf, send, recv, arrived=None):
        for side, present, piece, onward in self.spread_moves(s):
            @pl.when(present)
            def _():
                if s > 0:
                    self.arrival(buf, side, piece, send, recv)

                @pl.when(onward)
                def _():
                    self.copy(buf, side, piece, send, recv).start()

                if s > 0 and arrived is not None:
                    arrived(piece)

    def spread_drain(self, buf, send, recv):
        for s in range(self.size):
            for side, present, piece, onward in self.spread_moves(s):
                @pl.when(present & onward)
                def _():
                    self.copy(buf, side, piece, send, recv).wait_send()


def kernel(sizes, slot_ref, trial_ref, tiles_hbm, out_ref,
           tiles, dense, flipped, xg, yg1, yg2, part0, part1, part2, acc, y1, zsum0, zsum2, xsum, pair_out, pair_in,
           tile_sem, xg_send, xg_recv, xp_send, xp_recv, zs0_send, zs0_recv, zg_send, zg_recv,
           pr_send, pr_recv, xs_send, xs_recv, yg_send, yg_recv, yp_send, yp_recv, zs2_send, zs2_recv):
    row_size, col_size, blocks, tile, slots, streams = sizes
    x_size = row_size // 2
    piece_rows = trial_ref.shape[2]
    row, col = lax.axis_index("row"), lax.axis_index("col")
    x, core = lax.div(row, 2), lax.rem(row, 2)
    sibling = {"row": row + 1 - 2 * core}
    zline = Line(col_size, col, lambda d: {"col": col + d})
    xline = Line(x_size, x, lambda d: {"row": row + 2 * d})
    shift = jnp.where(row == col, filter_center, 0.0).astype(F32)

    tile_copy = pltpu.make_async_copy(tiles_hbm.at[0, 0], tiles.at[pl.ds(0, slots)], tile_sem)
    tile_copy.start()

    barrier = pltpu.get_barrier_semaphore()
    pl.semaphore_signal(barrier, inc=1, device_id=sibling, device_id_type=MESH)
    for line in (zline, xline):
        for d, there in ((-1, line.place > 0), (1, line.place < line.size - 1)):
            @pl.when(there)
            def _():
                pl.semaphore_signal(barrier, inc=1, device_id=line.peer(d), device_id_type=MESH)
    peers = 1
    for line in (zline, xline):
        peers += (line.place > 0).astype(jnp.int32) + (line.place < line.size - 1).astype(jnp.int32)
    pl.semaphore_wait(barrier, peers)

    def pair_copy(src, dst, send, recv):
        return pltpu.make_async_remote_copy(
            src_ref=src, dst_ref=dst, send_sem=send, recv_sem=recv, device_id=sibling, device_id_type=MESH)

    def gather_row(buf, s, send, recv, psend, precv):
        mine = Rows(buf, s, core)

        def to_sibling(place):
            ref = buf.at[s, 2 * place + core]
            pair_copy(ref, ref, psend.at[s, place], precv.at[s, place]).start()

        for step in range(x_size):
            xline.spread_step(step, mine, send.at[s], recv.at[s], to_sibling)
            if step == 0:
                to_sibling(x)
            yield
        for place in range(x_size):
            ref = buf.at[s, 2 * place + 1 - core]
            pair_copy(ref, ref, psend.at[s, place], precv.at[s, place]).wait_recv()

    def gather_row_drain(buf, s, send, recv, psend, precv):
        xline.spread_drain(Rows(buf, s, core), send.at[s], recv.at[s])
        for place in range(x_size):
            ref = buf.at[s, 2 * place + core]
            pair_copy(ref, ref, psend.at[s, place], precv.at[s, place]).wait_send()

    def product(matrix, source, piece, s, target):
        count = min(piece_rows, 256)

        @pl.loop(0, piece_rows // count)
        def _(k):
            inside = pl.ds(pl.multiple_of(k * count, count), count)
            rows = pl.ds(pl.multiple_of(piece * piece_rows + k * count, count), count)
            panel = source[s].reshape(row_size * piece_rows, LANES)
            value = jnp.dot(matrix[rows, :], panel, preferred_element_type=F32)
            target[inside, :] = (value - shift * source[s, piece, inside, :].astype(F32)).astype(target.dtype)

    def build(matrix, turned):
        per = blocks // 4
        for quarter in range(4):
            @pl.loop(quarter * per * blocks // 4, (quarter + 1) * per * blocks // 4)
            def _(group):
                for inner in range(4):
                    place = group * 4 + inner
                    i, j = lax.div(place, blocks), lax.rem(place, blocks)
                    if turned:
                        value = tiles[slot_ref[j * blocks + i]].T
                    else:
                        value = tiles[slot_ref[place]]
                    rows = pl.ds(pl.multiple_of(i * tile, tile), tile)
                    lanes = pl.ds(pl.multiple_of(j * tile, tile), tile)
                    matrix[rows, lanes] = value
            yield

        @pl.loop(0, blocks)
        def _(i):
            at = pl.ds(pl.multiple_of(i * tile, tile), tile)
            value = tiles[slot_ref[blocks * blocks + i]]
            matrix[at, at] += value.T if turned else value
        yield

    def products_and_sums(s, matrix, source, part, buf, send, recv):
        for t in range(col_size):
            piece = jnp.where(t < col, t, col_size - 1 - t + col)
            product(matrix, source, piece, s, part.at[s, piece])
            if t < col_size - 1:
                zline.sum_step(t, buf.at[s], part.at[s], send.at[s], recv.at[s])
                yield

    def stream(s):
        lanes = slice(s * LANES, (s + 1) * LANES)
        xg[s, row] = trial_ref[0, 0, :, lanes]
        yield from gather_row(xg, s, xg_send, xg_recv, xp_send, xp_recv)
        yield
        yield from products_and_sums(s, dense, xg, part0, zsum0, zs0_send, zs0_recv)
        zline.sum_finish(zsum0.at[s], part0.at[s], zs0_send.at[s], zs0_recv.at[s], acc)
        value = acc[...] / filter_radius
        y1[s] = value
        yg1[s, col] = value.astype(BF16)
        for step in range(col_size):
            zline.spread_step(step, yg1.at[s], zg_send.at[s], zg_recv.at[s])
            yield
        for place in range(x_size):
            product(flipped, yg1, 2 * place + 1 - core, s, pair_out.at[s, place])
        pair = pair_copy(pair_out.at[s], pair_in.at[s], pr_send.at[s], pr_recv.at[s])
        pair.start()
        for place in range(x_size):
            product(flipped, yg1, 2 * place + core, s, part1.at[s, place])
        yield
        pair.wait_recv()
        part1[s] += pair_in[s].astype(F32)
        for t in range(x_size - 1):
            xline.sum_step(t, xsum.at[s], part1.at[s], xs_send.at[s], xs_recv.at[s])
            yield
        xline.sum_finish(xsum.at[s], part1.at[s], xs_send.at[s], xs_recv.at[s], acc)
        value = (2.0 / filter_radius) * acc[...] - trial_ref[0, 0, :, lanes].astype(F32)
        yg2[s, row] = value.astype(BF16)
        yield from gather_row(yg2, s, yg_send, yg_recv, yp_send, yp_recv)
        yield
        yield from products_and_sums(s, dense, yg2, part2, zsum2, zs2_send, zs2_recv)
        zline.sum_finish(zsum2.at[s], part2.at[s], zs2_send.at[s], zs2_recv.at[s], acc)
        out_ref[0, 0, :, lanes] = (2.0 / filter_radius) * acc[...] - y1[s]

    def stream_drain(s):
        gather_row_drain(xg, s, xg_send, xg_recv, xp_send, xp_recv)
        zline.sum_drain(zsum0.at[s], zs0_send.at[s], zs0_recv.at[s])
        zline.spread_drain(yg1.at[s], zg_send.at[s], zg_recv.at[s])
        pair_copy(pair_out.at[s], pair_in.at[s], pr_send.at[s], pr_recv.at[s]).wait_send()
        xline.sum_drain(xsum.at[s], xs_send.at[s], xs_recv.at[s])
        gather_row_drain(yg2, s, yg_send, yg_recv, yp_send, yp_recv)
        zline.sum_drain(zsum2.at[s], zs2_send.at[s], zs2_recv.at[s])

    programs = [stream(s) for s in range(streams)]

    def advance(which, count=1):
        for _ in range(count):
            next(which, None)

    first = programs[0]
    advance(first)
    for other in programs[1:]:
        advance(other)
    tiles[slots] = jnp.zeros((tile, tile), BF16)
    tile_copy.wait()
    for _ in build(dense, False):
        pass
    turned = build(flipped, True)
    gathers = x_size
    advance(first, gathers)
    sums = col_size - 1
    advance(first)
    for other in programs[1:]:
        advance(other, gathers)
    advance(turned)
    for _ in range(sums - 1):
        advance(first)
        advance(turned)
    advance(first)
    for _ in turned:
        pass
    for _ in range(col_size - 1):
        for other in programs[1:]:
            advance(other)
        advance(first)
    advance(first)
    live = [True] * streams
    while any(live):
        for s in list(range(1, streams)) + [0]:
            if live[s]:
                try:
                    next(programs[s])
                except StopIteration:
                    live[s] = False
    for s in range(streams):
        stream_drain(s)


class Rows:
    def __init__(self, buf, s, core):
        self.buf, self.s, self.core = buf, s, core

    @property
    def at(self):
        return self

    def __getitem__(self, place):
        return self.buf.at[self.s, 2 * place + self.core]


def slot_table(rows, cols, count, blocks, slots):
    order = lax.iota(jnp.int32, slots)
    place = jnp.where(order < count, rows * blocks + cols, -1)
    hit = place[None, :] == lax.iota(jnp.int32, blocks * blocks)[:, None]
    first = jnp.min(jnp.where(hit, order[None, :], slots), axis=1)
    diagonal = lax.iota(jnp.int32, blocks) * (blocks + 1)
    hit = place[None, :] == diagonal[:, None]
    low = jnp.min(jnp.where(hit, order[None, :], slots), axis=1)
    high = jnp.max(jnp.where(hit, order[None, :], -1), axis=1)
    second = jnp.where(high > low, high, slots)
    return jnp.concatenate([first, second])


def per_device(trial_panel, tile_values, tile_rows, tile_cols, tile_counts):
    row_size, col_size = lax.axis_size("row"), lax.axis_size("col")
    piece_rows, vectors = trial_panel.shape[2:]
    slots, tile = tile_values.shape[2:4]
    blocks = piece_rows * row_size // tile
    order = piece_rows * row_size
    streams = vectors // LANES
    x_size = row_size // 2
    table = slot_table(tile_rows[0, 0], tile_cols[0, 0], tile_counts[0, 0], blocks, slots)
    piece = (piece_rows, LANES)

    def vmem(shape, dtype=BF16):
        return pltpu.VMEM(shape, dtype)

    def sems(*shape):
        return [pltpu.SemaphoreType.DMA(shape)] * 2

    scratch = [
        vmem((slots + 1, tile, tile)), vmem((order, order)), vmem((order, order)),
        vmem((streams, row_size) + piece), vmem((streams, col_size) + piece), vmem((streams, row_size) + piece),
        vmem((streams, col_size) + piece, F32), vmem((streams, x_size) + piece, F32),
        vmem((streams, col_size) + piece, F32), vmem(piece, F32), vmem((streams,) + piece, F32),
        vmem((streams, 2, col_size) + piece), vmem((streams, 2, col_size) + piece),
        vmem((streams, 2, x_size) + piece),
        vmem((streams, x_size) + piece), vmem((streams, x_size) + piece),
        pltpu.SemaphoreType.DMA,
        *sems(streams, 2, x_size), *sems(streams, x_size),
        *sems(streams, 2, col_size), *sems(streams, 2, col_size),
        *sems(streams), *sems(streams, 2, x_size),
        *sems(streams, 2, x_size), *sems(streams, x_size),
        *sems(streams, 2, col_size),
    ]
    sizes = (row_size, col_size, blocks, tile, slots, streams)
    return pl.pallas_call(
        functools.partial(kernel, sizes),
        out_shape=jax.ShapeDtypeStruct((1, 1, piece_rows, vectors), F32),
        in_specs=[pl.BlockSpec(memory_space=pltpu.SMEM), pl.BlockSpec(memory_space=pltpu.VMEM),
                  pl.BlockSpec(memory_space=pl.ANY)],
        out_specs=pl.BlockSpec(memory_space=pltpu.VMEM),
        scratch_shapes=scratch,
        compiler_params=pltpu.CompilerParams(
            collective_id=0, has_side_effects=True, vmem_limit_bytes=56 * 1024 * 1024),
        cost_estimate=pl.CostEstimate(
            flops=6 * order * order * vectors, bytes_accessed=slots * tile * tile * 2, transcendentals=0),
    )(table, trial_panel, tile_values)


def solution(mesh):
    return jax.shard_map(
        per_device,
        mesh=mesh,
        in_specs=(
            P(("groups", "col"), "row", None, None),
            P(("groups", "row"), "col", None, None, None),
            P(("groups", "row"), "col", None),
            P(("groups", "row"), "col", None),
            P(("groups", "row"), "col"),
        ),
        out_specs=P(("groups", "row"), "col", None, None),
        check_vma=False,
    )
```

```python
import functools

import jax
import jax.numpy as jnp
from jax import lax
from jax.experimental import pallas as pl
from jax.experimental.pallas import tpu as pltpu
from jax.sharding import PartitionSpec as P

MESH = pl.DeviceIdType.MESH
LANES = 128
filter_center = 0.5
filter_radius = 1.5
F32 = jnp.float32
BF16 = jnp.bfloat16


class Peers:
    def __init__(self, size, place, device):
        self.size, self.place, self.device = size, place, device

    def others(self):
        for d in range(1, self.size):
            yield lax.rem(self.place + d, self.size)

    def copy(self, src, dst, to, send, recv):
        return pltpu.make_async_remote_copy(
            src_ref=src, dst_ref=dst, send_sem=send, recv_sem=recv,
            device_id=self.device(to), device_id_type=MESH)

    def spread(self, buf, send, recv):
        here = buf(self.place)
        for peer in self.others():
            self.copy(here, here, peer, send.at[peer], recv.at[self.place]).start()

    def spread_wait(self, buf, send, recv, peer):
        self.copy(buf(peer), buf(peer), peer, send.at[peer], recv.at[peer]).wait_recv()

    def spread_drain(self, buf, send, recv):
        for peer in self.others():
            self.copy(buf(peer), buf(peer), peer, send.at[peer], recv.at[peer]).wait_send()

    def give(self, outgoing, incoming, to, send, recv):
        self.copy(outgoing.at[to], incoming.at[self.place], to, send.at[to], recv.at[self.place]).start()

    def collect(self, outgoing, incoming, own, send, recv):
        total = own
        for peer in self.others():
            self.copy(outgoing.at[peer], incoming.at[peer], peer, send.at[peer], recv.at[peer]).wait_recv()
            total = total + incoming[peer].astype(F32)
        return total

    def give_drain(self, outgoing, incoming, send, recv):
        for peer in self.others():
            self.copy(outgoing.at[peer], incoming.at[peer], peer, send.at[peer], recv.at[peer]).wait_send()


def kernel(sizes, slot_ref, trial_ref, tiles_hbm, out_ref,
           tiles, dense, flipped, xg, yg1, yg2, own, part1, y1, zout0, zin0, zout2, zin2, zrel0, zrel2, xout, xin, pair_out, pair_in,
           tile_sem, xg_send, xg_recv, xp_send, xp_recv, zs0_send, zs0_recv, zg_send, zg_recv,
           pr_send, pr_recv, xs_send, xs_recv, yg_send, yg_recv, yp_send, yp_recv, zs2_send, zs2_recv,
           zr0_recv, zr2_recv, zf_send):
    row_size, col_size, blocks, tile, slots, streams = sizes
    x_size = row_size // 2
    piece_rows = trial_ref.shape[2]
    row, col = lax.axis_index("row"), lax.axis_index("col")
    x, core = lax.div(row, 2), lax.rem(row, 2)
    sibling = {"row": row + 1 - 2 * core}
    zline = Peers(col_size, col, lambda i: {"col": i})
    xline = Peers(x_size, x, lambda i: {"row": 2 * i + core})
    shift = jnp.where(row == col, filter_center, 0.0).astype(F32)

    tile_copy = pltpu.make_async_copy(tiles_hbm.at[0, 0], tiles.at[pl.ds(0, slots)], tile_sem)
    tile_copy.start()

    barrier = pltpu.get_barrier_semaphore()
    pl.semaphore_signal(barrier, inc=1, device_id=sibling, device_id_type=MESH)
    for line in (zline, xline):
        for peer in line.others():
            pl.semaphore_signal(barrier, inc=1, device_id=line.device(peer), device_id_type=MESH)
    pl.semaphore_wait(barrier, col_size + x_size - 1)

    def pair_copy(src, dst, send, recv):
        return pltpu.make_async_remote_copy(
            src_ref=src, dst_ref=dst, send_sem=send, recv_sem=recv, device_id=sibling, device_id_type=MESH)

    def gather_row(buf, s, send, recv, psend, precv):
        def mine(place):
            return buf.at[s, 2 * place + core]

        def to_sibling(place):
            pair_copy(mine(place), mine(place), psend.at[s, place], precv.at[s, place]).start()

        xline.spread(mine, send.at[s], recv.at[s])
        to_sibling(x)
        yield
        for peer in xline.others():
            xline.spread_wait(mine, send.at[s], recv.at[s], peer)
            to_sibling(peer)
        yield
        for place in range(x_size):
            ref = buf.at[s, 2 * place + 1 - core]
            pair_copy(ref, ref, psend.at[s, place], precv.at[s, place]).wait_recv()

    def gather_row_drain(buf, s, send, recv, psend, precv):
        def mine(place):
            return buf.at[s, 2 * place + core]

        xline.spread_drain(mine, send.at[s], recv.at[s])
        for place in range(x_size):
            pair_copy(mine(place), mine(place), psend.at[s, place], precv.at[s, place]).wait_send()

    def product(matrix, source, piece, s, target):
        count = min(piece_rows, 256)

        @pl.loop(0, piece_rows // count)
        def _(k):
            inside = pl.ds(pl.multiple_of(k * count, count), count)
            rows = pl.ds(pl.multiple_of(piece * piece_rows + k * count, count), count)
            panel = source[s].reshape(row_size * piece_rows, LANES)
            value = jnp.dot(matrix[rows, :], panel, preferred_element_type=F32)
            target[inside, :] = (value - shift * source[s, piece, inside, :].astype(F32)).astype(target.dtype)

    def build(matrix, turned):
        per = blocks // 4
        for quarter in range(4):
            @pl.loop(quarter * per * blocks // 4, (quarter + 1) * per * blocks // 4)
            def _(group):
                for inner in range(4):
                    place = group * 4 + inner
                    i, j = lax.div(place, blocks), lax.rem(place, blocks)
                    if turned:
                        value = tiles[slot_ref[j * blocks + i]].T
                    else:
                        value = tiles[slot_ref[place]]
                    rows = pl.ds(pl.multiple_of(i * tile, tile), tile)
                    lanes = pl.ds(pl.multiple_of(j * tile, tile), tile)
                    matrix[rows, lanes] = value
            yield

        @pl.loop(0, blocks)
        def _(i):
            at = pl.ds(pl.multiple_of(i * tile, tile), tile)
            value = tiles[slot_ref[blocks * blocks + i]]
            matrix[at, at] += value.T if turned else value
        yield

    half = col_size // 2
    low = col < half
    base, gate = jnp.where(low, 0, half), jnp.where(low, half - 1, half)
    far_base, far_gate = jnp.where(low, half, 0), jnp.where(low, half, half - 1)
    at_gate = col == gate
    side = jnp.where(low, 0, 1)
    near = [lax.rem(col - base + d, half) + base for d in range(1, half)]

    def products_given(s, source, outgoing, relayed, incoming, send, recv, rsend, rrecv):
        for k in range(half):
            piece = far_base + k
            product(dense, source, piece, s, outgoing.at[s, piece])

            @pl.when(jnp.logical_not(at_gate))
            def _():
                place = col - base - side
                zline.copy(outgoing.at[s, piece], relayed.at[s, place, k], gate, send.at[s, piece],
                           rrecv.at[s, place, k]).start()
        for peer in near:
            product(dense, source, peer, s, outgoing.at[s, peer])
            zline.copy(outgoing.at[s, peer], incoming.at[s, col], peer, send.at[s, peer], recv.at[s, col]).start()
        product(dense, source, col, s, own.at[s])

    def relay_sums(s, outgoing, relayed, incoming, send, recv, rsend, rrecv):
        @pl.when(at_gate)
        def _():
            for k in range(half):
                piece = far_base + k
                total = outgoing[s, piece].astype(F32)
                for place in range(half - 1):
                    ref = relayed.at[s, place, k]
                    zline.copy(outgoing.at[s, piece], ref, far_gate, send.at[s, piece], rrecv.at[s, place, k]).wait_recv()
                    total = total + relayed[s, place, k].astype(F32)
                outgoing[s, piece] = total.astype(BF16)
                zline.copy(outgoing.at[s, piece], incoming.at[s, col], piece, send.at[s, piece], recv.at[s, col]).start()

    def collected(s, outgoing, incoming, send, recv):
        total = own[s]
        for peer in near + [far_gate]:
            zline.copy(outgoing.at[s, peer], incoming.at[s, peer], peer, send.at[s, peer], recv.at[s, peer]).wait_recv()
            total = total + incoming[s, peer].astype(F32)
        return total

    def given_drain(s, outgoing, incoming, send, recv):
        for piece in near + [far_base + k for k in range(half)]:
            zline.copy(outgoing.at[s, piece], incoming.at[s, piece], piece, send.at[s, piece], recv.at[s, piece]).wait_send()

    def spread_copy(s, piece, to, sem):
        return zline.copy(yg1.at[s, piece], yg1.at[s, piece], to, sem, zg_recv.at[s, piece])

    def spread_out(s):
        spread_copy(s, col, far_gate, zg_send.at[s, far_gate]).start()
        for peer in near:
            spread_copy(s, col, peer, zg_send.at[s, peer]).start()

    def relay_pieces(s):
        @pl.when(at_gate)
        def _():
            for k in range(half):
                piece = far_base + (k if half == 1 else jnp.where(low, k, half - 1 - k))
                spread_copy(s, piece, far_gate, zg_send.at[s, far_gate]).wait_recv()
                for place, peer in enumerate(near):
                    spread_copy(s, piece, peer, zf_send.at[s, k, place]).start()

    def spread_arrived(s):
        for peer in near:
            spread_copy(s, peer, peer, zg_send.at[s, peer]).wait_recv()

        @pl.when(jnp.logical_not(at_gate))
        def _():
            for k in range(half):
                spread_copy(s, far_base + k, gate, zg_send.at[s, far_gate]).wait_recv()

    def spread_out_drain(s):
        for peer in near + [far_gate]:
            spread_copy(s, col, peer, zg_send.at[s, peer]).wait_send()

        @pl.when(at_gate)
        def _():
            for k in range(half):
                for place, peer in enumerate(near):
                    spread_copy(s, far_base + k, peer, zf_send.at[s, k, place]).wait_send()

    def stream(s):
        lanes = slice(s * LANES, (s + 1) * LANES)
        xg[s, row] = trial_ref[0, 0, :, lanes]
        yield from gather_row(xg, s, xg_send, xg_recv, xp_send, xp_recv)
        first = (zout0, zrel0, zin0, zs0_send, zs0_recv, None, zr0_recv)
        products_given(s, xg, *first)
        yield
        relay_sums(s, *first)
        yield
        value = collected(s, zout0, zin0, zs0_send, zs0_recv) / filter_radius
        y1[s] = value
        yg1[s, col] = value.astype(BF16)
        spread_out(s)
        yield
        relay_pieces(s)
        yield
        spread_arrived(s)
        for place in range(x_size):
            product(flipped, yg1, 2 * place + 1 - core, s, pair_out.at[s, place])
        pair = pair_copy(pair_out.at[s], pair_in.at[s], pr_send.at[s], pr_recv.at[s])
        pair.start()
        for place in range(x_size):
            product(flipped, yg1, 2 * place + core, s, part1.at[s, place])
        yield
        pair.wait_recv()
        for peer in xline.others():
            xout[s, peer] = (part1[s, peer] + pair_in[s, peer].astype(F32)).astype(BF16)
            xline.give(xout.at[s], xin.at[s], peer, xs_send.at[s], xs_recv.at[s])
        yield
        value = part1[s, x] + pair_in[s, x].astype(F32)
        value = xline.collect(xout.at[s], xin.at[s], value, xs_send.at[s], xs_recv.at[s])
        value = (2.0 / filter_radius) * value - trial_ref[0, 0, :, lanes].astype(F32)
        yg2[s, row] = value.astype(BF16)
        yield from gather_row(yg2, s, yg_send, yg_recv, yp_send, yp_recv)
        last = (zout2, zrel2, zin2, zs2_send, zs2_recv, None, zr2_recv)
        products_given(s, yg2, *last)
        yield
        relay_sums(s, *last)
        yield
        value = collected(s, zout2, zin2, zs2_send, zs2_recv)
        out_ref[0, 0, :, lanes] = (2.0 / filter_radius) * value - y1[s]

    def stream_drain(s):
        gather_row_drain(xg, s, xg_send, xg_recv, xp_send, xp_recv)
        given_drain(s, zout0, zin0, zs0_send, zs0_recv)
        spread_out_drain(s)
        pair_copy(pair_out.at[s], pair_in.at[s], pr_send.at[s], pr_recv.at[s]).wait_send()
        xline.give_drain(xout.at[s], xin.at[s], xs_send.at[s], xs_recv.at[s])
        gather_row_drain(yg2, s, yg_send, yg_recv, yp_send, yp_recv)
        given_drain(s, zout2, zin2, zs2_send, zs2_recv)

    programs = [stream(s) for s in range(streams)]

    def advance(s):
        next(programs[s], None)

    for s in range(streams):
        advance(s)
    tiles[slots] = jnp.zeros((tile, tile), BF16)
    tile_copy.wait()
    for _ in build(dense, False):
        pass
    turned = build(flipped, True)
    for s in range(streams):
        advance(s)
    done, lag = [2] * streams, 1
    for turn in range(2, 13 + lag * (streams - 1)):
        for s in range(streams):
            if done[s] < 13 and turn >= 2 + lag * s:
                advance(s)
                done[s] += 1
        if turn < 5:
            next(turned, None)
        elif turn == 5:
            for _ in turned:
                pass
    for s in range(streams):
        stream_drain(s)


def slot_table(rows, cols, count, blocks, slots):
    order = lax.iota(jnp.int32, slots)
    place = jnp.where(order < count, rows * blocks + cols, -1)
    hit = place[None, :] == lax.iota(jnp.int32, blocks * blocks)[:, None]
    first = jnp.min(jnp.where(hit, order[None, :], slots), axis=1)
    diagonal = lax.iota(jnp.int32, blocks) * (blocks + 1)
    hit = place[None, :] == diagonal[:, None]
    low = jnp.min(jnp.where(hit, order[None, :], slots), axis=1)
    high = jnp.max(jnp.where(hit, order[None, :], -1), axis=1)
    second = jnp.where(high > low, high, slots)
    return jnp.concatenate([first, second])


def per_device(trial_panel, tile_values, tile_rows, tile_cols, tile_counts):
    row_size, col_size = lax.axis_size("row"), lax.axis_size("col")
    piece_rows, vectors = trial_panel.shape[2:]
    slots, tile = tile_values.shape[2:4]
    blocks = piece_rows * row_size // tile
    order = piece_rows * row_size
    streams = vectors // LANES
    x_size = row_size // 2
    table = slot_table(tile_rows[0, 0], tile_cols[0, 0], tile_counts[0, 0], blocks, slots)
    piece = (piece_rows, LANES)
    relay = (max(col_size // 2 - 1, 1), col_size // 2)

    def vmem(shape, dtype=BF16):
        return pltpu.VMEM(shape, dtype)

    def sems(*shape):
        return [pltpu.SemaphoreType.DMA(shape)] * 2

    scratch = [
        vmem((slots + 1, tile, tile)), vmem((order, order)), vmem((order, order)),
        vmem((streams, row_size) + piece), vmem((streams, col_size) + piece), vmem((streams, row_size) + piece),
        vmem((streams,) + piece, F32), vmem((streams, x_size) + piece, F32), vmem((streams,) + piece, F32),
        *[vmem((streams, col_size) + piece)] * 4,
        *[vmem((streams,) + relay + piece)] * 2,
        *[vmem((streams, x_size) + piece)] * 4,
        pltpu.SemaphoreType.DMA,
        *sems(streams, x_size), *sems(streams, x_size),
        *sems(streams, col_size), *sems(streams, col_size),
        *sems(streams), *sems(streams, x_size),
        *sems(streams, x_size), *sems(streams, x_size),
        *sems(streams, col_size),
        *sems(streams, *relay), pltpu.SemaphoreType.DMA((streams,) + relay[::-1]),
    ]
    sizes = (row_size, col_size, blocks, tile, slots, streams)
    return pl.pallas_call(
        functools.partial(kernel, sizes),
        out_shape=jax.ShapeDtypeStruct((1, 1, piece_rows, vectors), F32),
        in_specs=[pl.BlockSpec(memory_space=pltpu.SMEM), pl.BlockSpec(memory_space=pltpu.VMEM),
                  pl.BlockSpec(memory_space=pl.ANY)],
        out_specs=pl.BlockSpec(memory_space=pltpu.VMEM),
        scratch_shapes=scratch,
        compiler_params=pltpu.CompilerParams(
            collective_id=0, has_side_effects=True, vmem_limit_bytes=56 * 1024 * 1024),
        cost_estimate=pl.CostEstimate(
            flops=6 * order * order * vectors, bytes_accessed=slots * tile * tile * 2, transcendentals=0),
    )(table, trial_panel, tile_values)


def solution(mesh):
    return jax.shard_map(
        per_device,
        mesh=mesh,
        in_specs=(
            P(("groups", "col"), "row", None, None),
            P(("groups", "row"), "col", None, None, None),
            P(("groups", "row"), "col", None),
            P(("groups", "row"), "col", None),
            P(("groups", "row"), "col"),
        ),
        out_specs=P(("groups", "row"), "col", None, None),
        check_vma=False,
    )
```
